32 devices in a mesh: groups: 2 (over x), blk: 16 (over z, y, core).
Axes of the slice: x: 2, y: 2, z: 4, core: 2. Of those that a mesh axis runs over, the one named last changes fastest.
Arguments:
- pop_cells: bfloat16 [2048, 1024], P('blk', 'groups'), parts along dimension 1, may hold values from 0.0009994507 to 1
- cell_map: int32 [512], replicated, may hold values from 0 to 255, never falling along the last dimension, each value on 1 to 4 neighbouring positions
- line_level: int32 [524288], P('blk'), may hold values from 0 to 2047
- line_strength: float32 [524288], P('blk'), may hold values from 0.001 to 1
- inst_wave: float32 [129], replicated, may hold values from 0.002 to 0.02
- inst_slit: float32 [9], replicated, may hold values from 0.05 to 0.25
Outputs:
- image: float32 [512, 2048], P(('groups', 'blk')), parts along dimension 0
The draws below stay inside these ranges and needn't reach their ends.
There are 2 independent parts, one for each index of `groups`. The reference program is written for one: setup_inputs(seed, part) draws one part's arguments, and reference() takes and returns one part's arrays. A program takes and returns all parts, laid end to end along the dimension named above; an argument that names none is the same for every part. Nothing has to cross between parts.
All inputs are finite; a program needn't handle non-finite values.
Results may differ from the reference program's by a relative error of at most 0.0003.
Values may be sent and summed in bfloat16 or wider, within the bound.
No kernel may reach another device: no remote copies, remote signals or barrier semaphores. Data moves between devices by JAX's collectives and lax.ppermute only.
A program may use at most 128 MiB of HBM per device.

```python
import math
import jax
import jax.numpy as jnp
import numpy as np
from jax import lax

L = 2048
W_DEV = 1024
LINES_BIN = 32
WAVE_TAPS = 129
SLIT_TAPS = 9
C = 256
R = 512
W = 16384
NL_DEV = 32768
NL = 524288
N_BLK = 16


def plant(values, own_key, low, largest):
    shape = values.shape
    spot = [jax.random.randint(jax.random.fold_in(own_key, axis), (), 0, shape[axis]) for axis in range(len(shape))]
    values = values.at[tuple(spot)].set(low)
    longest = shape.index(max(shape))
    spot[longest] = (spot[longest] + 1) % shape[longest]
    return values.at[tuple(spot)].set(largest)


def level_of(own_key, extent, split, smallest, largest):
    loudness, own = 1.0, jax.random.fold_in(own_key, 6)
    for dim, blocks in split:
        steps = jnp.exp(jax.random.uniform(jax.random.fold_in(own, dim), (blocks,), jnp.float32, smallest / len(split), largest / len(split)))
        loudness = loudness * jnp.repeat(steps, extent[dim] // blocks).reshape([-1 if axis == dim else 1 for axis in range(len(extent))])
    return loudness


def profile(number_of, total, reach, lean):
    weights = [(1 << 20) // math.isqrt(rank ** lean) + 1 for rank in range(2, number_of + 1)]
    rest, holding = total - reach - (number_of - 1), [1] * (number_of - 1)
    while rest > 0:
        free = [i for i in range(number_of - 1) if holding[i] < reach]
        mass, remaining = sum([weights[i] for i in free]), rest
        for i in free:
            extra = min(reach - holding[i], max(1, remaining * weights[i] // mass), rest)
            holding[i] = holding[i] + extra
            rest = rest - extra
    return np.array([reach] + holding)


def ragged_sizes(rng, number_of, total, most, lean):
    if number_of == 2:
        one = jax.random.randint(rng, (), max(1, total - most), min(most, total - 1) + 1)
        return jnp.stack([one, total - one])
    sizes = jnp.asarray(profile(number_of, total, most, lean), jnp.int32)
    couples = (number_of - 1) // 2
    donor, sink = sizes[1:1 + 2 * couples:2], sizes[2:2 + 2 * couples:2]
    slack = jnp.minimum(donor - 1, most - sink)
    moved = jax.random.randint(jax.random.fold_in(rng, 1), (couples,), 0, 1 << 20) % (slack + 1)
    sizes = sizes.at[1:1 + 2 * couples:2].set(donor - moved).at[2:2 + 2 * couples:2].set(sink + moved)
    return sizes[jax.random.permutation(jax.random.fold_in(rng, 2), number_of)]


def setup_inputs(seed: int = 0, part: int = 0) -> dict:
    keys = jax.random.split(jax.random.key(seed), 7)
    part_keys = jax.random.split(jax.random.fold_in(keys[6], part), 7)
    pop_cells = jnp.clip(jnp.exp(math.log(1.0) - 6.9083047 * jax.random.uniform(part_keys[0], (L, R), jnp.float32) ** level_of(part_keys[0], (L, R), ((0, 16),), -0.2, 0.2)), 0.0009994507, 1.0).astype(jnp.bfloat16)
    cell_map = jnp.searchsorted(jnp.cumsum(ragged_sizes(keys[1], C, R, 4, 0)), jnp.arange(R), side="right").astype(jnp.int32)
    line_level = plant(jax.random.randint(keys[2], (NL,), 0, L), jax.random.fold_in(keys[2], 1), 0, L - 1).astype(jnp.int32)
    line_strength = jnp.clip(jnp.exp(math.log(1.0) - 6.9077552 * jax.random.uniform(keys[3], (NL,), jnp.float32) ** level_of(keys[3], (NL,), ((0, 16),), -0.2, 0.2)), 0.001, 1.0)
    inst_wave = jnp.clip(jnp.exp(jax.random.uniform(keys[4], (WAVE_TAPS,), jnp.float32, math.log(0.002), math.log(0.02))), 0.002, 0.02)
    inst_slit = jnp.clip(jnp.exp(jax.random.uniform(keys[5], (SLIT_TAPS,), jnp.float32, math.log(0.05), math.log(0.25))), 0.05, 0.25)
    return {"pop_cells": pop_cells, "cell_map": cell_map, "line_level": line_level, "line_strength": line_strength, "inst_wave": inst_wave, "inst_slit": inst_slit}


def smear(padded, inst_wave):
    cells = padded.shape[0]
    width = padded.shape[1]
    outputs = (width - 128) // 8
    blocks = jnp.concatenate([inst_wave, jnp.zeros((7,), inst_wave.dtype)]).reshape(17, 8)
    parts = jnp.transpose(padded.reshape(cells, width // 8, 8), (2, 0, 1))
    total = jnp.zeros((cells, outputs), padded.dtype)
    for block_index in range(17):
        window = parts[:, :, block_index:block_index + outputs]
        total = total + jnp.einsum("i,icb->cb", blocks[block_index], window, precision=lax.Precision.HIGHEST)
    return total


def slit_blur(smeared, inst_slit):
    cells = smeared.shape[0]
    padded = jnp.pad(smeared, ((4, 4), (0, 0)))
    total = inst_slit[0] * padded[0:cells]
    for tap_index in range(1, 9):
        total = total + inst_slit[tap_index] * padded[tap_index:tap_index + cells]
    return total


def reference(pop_cells, cell_map, line_level, line_strength, inst_wave, inst_slit):
    onehot = (cell_map[:, None] == jnp.arange(C, dtype=jnp.int32)[None, :]).astype(jnp.bfloat16)
    slit_pop = jnp.dot(pop_cells, onehot, preferred_element_type=jnp.float32).astype(jnp.bfloat16)
    width = W_DEV + 128
    line_bin = (jnp.arange(NL, dtype=jnp.int32) // LINES_BIN).astype(jnp.int32)

    def one_tile(tile):
        levels = []
        places = []
        weights = []
        for neighbour in (-1, 0, 1):
            source = tile + neighbour
            present = (source >= 0) & (source < N_BLK)
            first = (jnp.clip(source, 0, N_BLK - 1) * NL_DEV).astype(jnp.int32)
            level_part = lax.dynamic_slice_in_dim(line_level, first, NL_DEV)
            bin_part = lax.dynamic_slice_in_dim(line_bin, first, NL_DEV)
            strength_part = lax.dynamic_slice_in_dim(line_strength, first, NL_DEV)
            relative = bin_part - (tile * W_DEV - 64)
            valid = present & (relative >= 0) & (relative < width)
            levels.append(level_part)
            places.append(jnp.where(valid, relative, width).astype(jnp.int32))
            weights.append(jnp.where(valid, strength_part, jnp.zeros((), line_strength.dtype)))
        emission = jnp.zeros((L, width + 1), jnp.float32)
        emission = emission.at[jnp.concatenate(levels), jnp.concatenate(places)].add(jnp.concatenate(weights))
        emission = emission[:, :width].astype(jnp.bfloat16)
        spectrum = lax.dot_general(slit_pop, emission, (((0,), (0,)), ((), ())), preferred_element_type=jnp.float32)
        smeared = smear(spectrum, inst_wave)
        return slit_blur(smeared, inst_slit)

    tiles = lax.map(one_tile, jnp.arange(N_BLK, dtype=jnp.int32))
    return jnp.transpose(tiles, (1, 0, 2)).reshape(C, W // 8)
```

```python
import functools

import jax
import jax.numpy as jnp
from jax import lax
from jax.experimental import pallas as pl
from jax.experimental.pallas import tpu as pltpu
from jax.sharding import PartitionSpec as P

L = 2048
LINES_BIN = 32
CELL_DEV = 16
SPLIT = (2, 2, 0)
LOW = 128
HIGH = L // LOW
BINS = 8
CHUNK = 256
REACH = 8
BF16 = jnp.bfloat16
F32 = jnp.float32
VMEM_LIMIT = 48 * 1024 * 1024
CONTRACT_LAST = (((1,), (1,)), ((), ()))


def two_terms(values):
    first = values.astype(BF16)
    return first, (values - first.astype(F32)).astype(BF16)


def emission_kernel(level_ref, strength_ref, wave_ref, out_ref, em_ref, *, first_chunk, chunks, unroll):
    outputs = CHUNK // BINS
    base = jnp.broadcast_to(wave_ref[...], (outputs + 2 * REACH, wave_ref.shape[1]))
    taps = pltpu.roll(base, wave_ref.shape[1] - 128, 1, stride=BINS, stride_axis=0)[:, :CHUNK]
    taps = jnp.concatenate(two_terms(taps), axis=0)
    rows = [
        (lax.broadcasted_iota(jnp.int32, (16, 128), 0) + 16 * block).astype(F32).astype(BF16)
        for block in range(LOW // 16)
    ]
    lane_bin = lax.broadcasted_iota(jnp.int32, (1, 128), 1) // LINES_BIN
    zero = jnp.zeros((16, 128), BF16)
    one = jnp.ones((16, 128), BF16)

    def spread(row):
        return jnp.broadcast_to(row.astype(F32), (16, 128)).astype(BF16)

    def half(index, part):
        level = level_ref[pl.ds(index, 1), :]
        high = spread((level // LOW) * BINS + (lane_bin + part * (128 // LINES_BIN)))
        low = spread(level % LOW)
        strength = spread(strength_ref[pl.ds(index, 1), :])
        a = jnp.concatenate([jnp.where(high == row, strength, zero) for row in rows], axis=0)
        b = jnp.concatenate([jnp.where(low == row, one, zero) for row in rows], axis=0)
        return a, b

    def group(index):
        a0, b0 = half(2 * index, 0)
        a1, b1 = half(2 * index + 1, 1)
        return lax.dot_general(
            jnp.concatenate([a0, a1], axis=1),
            jnp.concatenate([b0, b1], axis=1),
            CONTRACT_LAST,
            preferred_element_type=F32,
        )

    out_ref[...] = jnp.zeros_like(out_ref)
    groups = CHUNK // BINS
    for chunk in range(chunks):

        @pl.loop(0, groups // 2, unroll=unroll)
        def _(pair):
            index = (first_chunk + chunk) * groups + 2 * pair
            x = group(index)
            y = group(index + 1)
            place = pl.ds(pl.multiple_of(16 * pair, 16), 16)
            for h in range(HIGH):
                rows_h = slice(BINS * h, BINS * h + BINS)
                em_ref[place, h * LOW : (h + 1) * LOW] = jnp.concatenate(
                    [x[rows_h], y[rows_h]], axis=0
                ).astype(BF16)

        blurred = jnp.dot(taps, em_ref[...], preferred_element_type=F32)
        span = outputs + 2 * REACH
        out_ref[outputs * chunk : outputs * chunk + span, :] += blurred[:span] + blurred[span:]


def blurred_emission(level, strength, wave, first_chunk, chunks, unroll=4):
    outputs = CHUNK // BINS
    bins = level.size // LINES_BIN
    cost = pl.CostEstimate(
        flops=2 * chunks * CHUNK * L * (HIGH * BINS + 96), bytes_accessed=chunks * CHUNK * 256, transcendentals=0
    )
    return pl.pallas_call(
        functools.partial(emission_kernel, first_chunk=first_chunk, chunks=chunks, unroll=unroll),
        out_shape=jax.ShapeDtypeStruct((outputs * chunks + 2 * REACH, L), F32),
        scratch_shapes=[pltpu.VMEM((CHUNK, L), BF16)],
        compiler_params=pltpu.CompilerParams(vmem_limit_bytes=VMEM_LIMIT),
        cost_estimate=cost,
        name="emission",
    )(level, strength, wave)


def image_kernel(slit_ref, pop_ref, *refs, starts):
    part_refs = refs[: len(starts)]
    out_ref, e_ref, pad_ref = refs[len(starts) :]
    cells = pop_ref.shape[0]
    outputs = out_ref.shape[1] - 128
    e_ref[...] = jnp.zeros_like(e_ref)
    for start, part_ref in zip(starts, part_refs):
        e_ref[start : start + part_ref.shape[0], :] += part_ref[...]
    rows = jnp.concatenate(
        [
            e_ref[REACH : REACH + outputs, :],
            e_ref[REACH + outputs :, :],
            jnp.zeros((128 - 2 * REACH, e_ref.shape[1]), F32),
            e_ref[:REACH, :],
        ],
        axis=0,
    )
    first, second = two_terms(rows)
    smeared = lax.dot_general(pop_ref[...], first, CONTRACT_LAST, preferred_element_type=F32)
    smeared += lax.dot_general(pop_ref[...], second, CONTRACT_LAST, preferred_element_type=F32)
    pad_ref[...] = jnp.zeros_like(pad_ref)
    pad_ref[8 : 8 + cells, :] = smeared
    total = slit_ref[0] * pad_ref[4 : 4 + cells, :]
    for tap in range(1, 9):
        total += slit_ref[tap] * pad_ref[4 + tap : 4 + tap + cells, :]
    out_ref[...] = total


def partial_image(pop, parts, starts, slit, outputs):
    cells = pop.shape[0]
    vmem = pl.BlockSpec(memory_space=pltpu.VMEM)
    return pl.pallas_call(
        functools.partial(image_kernel, starts=starts),
        out_shape=jax.ShapeDtypeStruct((cells, outputs + 128), F32),
        in_specs=[pl.BlockSpec(memory_space=pltpu.SMEM)] + [vmem] * (1 + len(parts)),
        scratch_shapes=[
            pltpu.VMEM((outputs + 2 * REACH, L), F32),
            pltpu.VMEM((cells + 16, outputs + 128), F32),
        ],
        compiler_params=pltpu.CompilerParams(vmem_limit_bytes=VMEM_LIMIT),
        cost_estimate=pl.CostEstimate(flops=4 * cells * L * (outputs + 128), bytes_accessed=cells * L * 2, transcendentals=0),
        name="image",
    )(slit, pop, *parts)


def swap(values, offset, count):
    return lax.ppermute(values, "blk", [(i, i ^ offset) for i in range(count)])


def gather_steps(count):
    steps = []
    offset = count
    while offset > 4:
        size = min(4, offset // 4)
        offset //= size
        steps.append([offset * i for i in range(1, size)])
    while offset > 1:
        offset //= 2
        steps.append([offset])
    return steps


def gathered_level(level, steps, own_levels):
    owner = (level // own_levels) ^ lax.axis_index("blk")
    position = jnp.zeros_like(level)
    blocks = 1
    for offsets in steps:
        size = len(offsets) + 1
        position += ((owner // offsets[0]) % size) * blocks
        blocks *= size
    return position * own_levels + level % own_levels


def body(pop_cells, cell_map, line_level, line_strength, inst_wave, inst_slit):
    count = lax.axis_size("blk")
    own_levels = pop_cells.shape[0]
    bins = line_level.shape[0] // LINES_BIN
    outputs, chunks = bins // BINS, bins // CHUNK
    cells = CELL_DEV * count
    steps = gather_steps(count)

    onehot = (cell_map[None, :] == jnp.arange(cells, dtype=jnp.int32)[:, None]).astype(BF16)
    pop = lax.dot_general(onehot, pop_cells, CONTRACT_LAST, preferred_element_type=F32).astype(BF16)

    level = gathered_level(line_level, steps, own_levels).reshape(-1, 128)
    strength = line_strength.reshape(-1, 128)
    wave = jnp.pad(inst_wave, (0, 512 - inst_wave.shape[0])).reshape(1, 512)
    part_steps = SPLIT
    parts, starts = [], []
    first = 0
    for index, offsets in enumerate(steps):
        pieces = [pop] + [swap(pop, k, count) for k in offsets]
        place = index - (len(steps) - 3)
        if place >= 0 and part_steps[place]:
            parts.append(blurred_emission(level, strength, wave, first, part_steps[place]))
            starts.append(first * (CHUNK // BINS))
            first += part_steps[place]
            pieces, parts[-1] = lax.optimization_barrier((pieces, parts[-1]))
        pop = jnp.concatenate(pieces, axis=1)
    wide = partial_image(pop, parts, starts, inst_slit, outputs)
    got = lax.all_to_all(wide, "blk", split_axis=0, concat_axis=0, tiled=True)
    got = got.reshape(count, CELL_DEV, outputs + 128)
    lane = jnp.arange(outputs)
    after = jnp.pad(jnp.where(lane < REACH, got[:-1, :, outputs:], 0), ((1, 0), (0, 0), (0, 0)))
    before = jnp.pad(jnp.where(lane >= outputs - REACH, got[1:, :, outputs:], 0), ((0, 1), (0, 0), (0, 0)))
    image = got[:, :, :outputs] + after + before
    return jnp.transpose(image, (1, 0, 2)).reshape(CELL_DEV, count * outputs)


def solution(mesh):
    placed = (P("blk", "groups"), P(), P("blk"), P("blk"), P(), P())
    return jax.shard_map(
        body, mesh=mesh, in_specs=placed, out_specs=P(("groups", "blk"), None), check_vma=False
    )
```

```python
import functools

import jax
import jax.numpy as jnp
from jax import lax
from jax.experimental import pallas as pl
from jax.experimental.pallas import tpu as pltpu
from jax.sharding import PartitionSpec as P

L = 2048
LINES_BIN = 32
CELL_DEV = 16
LOW = 128
HIGH = L // LOW
BINS = 8
CHUNK = 256
REACH = 8
CHUNK_OUT = CHUNK // BINS
SPAN = CHUNK_OUT + 2 * REACH
CHUNK_ROWS = CHUNK * LINES_BIN // 128
TAP_WIDTH = 512
UNROLL = 4
BF16 = jnp.bfloat16
F32 = jnp.float32
VMEM_LIMIT = 48 * 1024 * 1024
CONTRACT_LAST = (((1,), (1,)), ((), ()))
VMEM = pl.BlockSpec(memory_space=pltpu.VMEM)
SMEM = pl.BlockSpec(memory_space=pltpu.SMEM)


def two_terms(values):
    first = values.astype(BF16)
    return first, (values - first.astype(F32)).astype(BF16)


def tap_matrix(wave_ref, tap_ref):
    tap_ref[...] = jnp.zeros_like(tap_ref)
    tap_ref[:, : wave_ref.shape[1]] = jnp.broadcast_to(wave_ref[...], (8, wave_ref.shape[1]))
    base = jnp.concatenate([tap_ref[...]] * (SPAN // 8), axis=0)
    taps = pltpu.roll(base, TAP_WIDTH - 128, 1, stride=BINS, stride_axis=0)[:, :CHUNK]
    return taps


def emission(lines, own_levels, scratch):
    level_ref, strength_ref, first_row, rows = lines
    high_ref, low_ref, em_ref = scratch
    level = level_ref[first_row : first_row + rows, :].astype(jnp.int32)
    owner = level // own_levels
    row_bin = lax.broadcasted_iota(jnp.int32, (rows, 128), 0) % 2 * (128 // LINES_BIN)
    lane_bin = lax.broadcasted_iota(jnp.int32, (rows, 128), 1) // LINES_BIN
    high_ref[:rows, :] = (owner % HIGH * BINS + row_bin + lane_bin).astype(F32)
    low_ref[:rows, :] = (owner // HIGH * own_levels + level % own_levels).astype(F32)

    choices = [
        (lax.broadcasted_iota(jnp.int32, (16, 128), 0) + 16 * block).astype(F32).astype(BF16)
        for block in range(LOW // 16)
    ]
    zero = jnp.zeros((16, 128), BF16)
    one = jnp.ones((16, 128), BF16)

    def spread(ref, index):
        return jnp.broadcast_to(ref[pl.ds(index, 1), :], (16, 128)).astype(BF16)

    def half(index):
        high = spread(high_ref, index)
        low = spread(low_ref, index)
        strength = spread(strength_ref, first_row + index)
        a = jnp.concatenate([jnp.where(high == choice, strength, zero) for choice in choices], axis=0)
        b = jnp.concatenate([jnp.where(low == choice, one, zero) for choice in choices], axis=0)
        return a, b

    def group(index):
        a0, b0 = half(2 * index)
        a1, b1 = half(2 * index + 1)
        return lax.dot_general(
            jnp.concatenate([a0, a1], axis=1),
            jnp.concatenate([b0, b1], axis=1),
            CONTRACT_LAST,
            preferred_element_type=F32,
        )

    @pl.loop(0, rows // 4, unroll=UNROLL)
    def _(pair):
        x = group(2 * pair)
        y = group(2 * pair + 1)
        place = pl.ds(pl.multiple_of(16 * pair, 16), 16)
        for h in range(HIGH):
            own = slice(BINS * h, BINS * h + BINS)
            em_ref[place, h * LOW : (h + 1) * LOW] = jnp.concatenate([x[own], y[own]], axis=0).astype(BF16)


def blurred(taps, em):
    rows = taps.shape[0]
    both = jnp.dot(jnp.concatenate(two_terms(taps), axis=0), em, preferred_element_type=F32)
    return both[:rows] + both[rows:]


def add_chunks(total_ref, chunks, taps, level_ref, strength_ref, own_levels, scratch):
    for chunk in chunks:
        emission((level_ref, strength_ref, chunk * CHUNK_ROWS, CHUNK_ROWS), own_levels, scratch)
        place = slice(chunk * CHUNK_OUT, chunk * CHUNK_OUT + SPAN)
        total_ref[place, :] += blurred(taps, scratch[-1][...])


def first_kernel(level_ref, strength_ref, wave_ref, total_ref, tap_ref, *scratch, chunks, own_levels):
    total_ref[...] = jnp.zeros_like(total_ref)
    taps = tap_matrix(wave_ref, tap_ref)
    add_chunks(total_ref, chunks, taps, level_ref, strength_ref, own_levels, scratch)


def last_kernel(
    level_ref, strength_ref, wave_ref, given_ref, out_ref, total_ref, tap_ref, *scratch, chunks, own_levels
):
    outputs = total_ref.shape[0] - 2 * REACH
    total_ref[...] = given_ref[...]
    taps = tap_matrix(wave_ref, tap_ref)
    add_chunks(total_ref, chunks, taps, level_ref, strength_ref, own_levels, scratch)
    first, second = two_terms(total_ref[REACH : REACH + outputs, :])
    out_ref[:outputs, :] = first
    out_ref[outputs : 2 * outputs, :] = second
    edges = jnp.concatenate([total_ref[REACH + outputs :, :], total_ref[:REACH, :]], axis=0)
    first, second = two_terms(edges)
    out_ref[2 * outputs : 2 * outputs + 2 * REACH, :] = first
    out_ref[2 * outputs + 2 * REACH :, :] = second


def emission_call(kernel, out_shape, operands, chunks, extra=()):
    scratch = [
        pltpu.VMEM((8, TAP_WIDTH), F32),
        pltpu.VMEM((CHUNK_ROWS, 128), F32),
        pltpu.VMEM((CHUNK_ROWS, 128), F32),
        pltpu.VMEM((CHUNK, L), BF16),
    ]
    return pl.pallas_call(
        kernel,
        out_shape=out_shape,
        in_specs=[VMEM] * len(operands),
        scratch_shapes=list(extra) + scratch,
        compiler_params=pltpu.CompilerParams(vmem_limit_bytes=VMEM_LIMIT),
        cost_estimate=pl.CostEstimate(
            flops=2 * chunks * CHUNK * L * 1024, bytes_accessed=chunks * CHUNK * 256, transcendentals=0
        ),
        name="emission",
    )(*operands)


def products(total, terms_ref, pop_refs, offsets):
    me = lax.axis_index("blk") % HIGH

    def block(offset):
        return terms_ref[:, pl.ds(pl.multiple_of((me ^ offset) * LOW, LOW), LOW)]

    for pop_ref, own in zip(pop_refs, offsets):
        for i in range(0, len(own), 2):
            terms = jnp.concatenate([block(own[i]), block(own[i + 1])], axis=1)
            pop = pop_ref[:, i * LOW : (i + 2) * LOW]
            new = lax.dot_general(pop, terms, CONTRACT_LAST, preferred_element_type=F32)
            total = new if total is None else total + new
    return total


def early_kernel(terms_ref, *refs, offsets):
    refs[-1][...] = products(None, terms_ref, refs[:-1], offsets)


def image_kernel(slit_ref, terms_ref, given_ref, *refs, offsets):
    pop_refs, (out_ref, pad_ref) = refs[:-2], refs[-2:]
    cells, outputs = pop_refs[0].shape[0], out_ref.shape[2]
    total = products(given_ref[...], terms_ref, pop_refs, offsets)
    edge = 2 * REACH
    pad_ref[:8, :] = jnp.zeros((8, pad_ref.shape[1]), F32)
    pad_ref[8 + cells :, :] = jnp.zeros((8, pad_ref.shape[1]), F32)
    pad_ref[8 : 8 + cells, :outputs] = total[:, :outputs] + total[:, outputs : 2 * outputs]
    pad_ref[8 : 8 + cells, outputs : outputs + edge] = (
        total[:, 2 * outputs : 2 * outputs + edge] + total[:, 2 * outputs + edge :]
    )
    image = slit_ref[0] * pad_ref[4 : 4 + cells, :]
    for tap in range(1, 9):
        image += slit_ref[tap] * pad_ref[4 + tap : 4 + tap + cells, :]
    lane = lax.broadcasted_iota(jnp.int32, (8, 128), 1)
    for place in range(cells // CELL_DEV):
        own = image[place * CELL_DEV : (place + 1) * CELL_DEV]
        out_ref[place, :CELL_DEV, :] = own[:, :outputs]
        moved = pltpu.roll(own[8:, outputs:], edge, 1)
        out_ref[place, CELL_DEV:, :] = jnp.where(lane < edge, own[:8, outputs:], moved)


def join(got):
    count, outputs = got.shape[0], got.shape[2]
    edge = got[:, CELL_DEV:, :]
    after = jnp.concatenate([edge[:-1, :, :REACH], edge[:-1, :, 2 * REACH : 3 * REACH]], axis=1)
    before = jnp.concatenate([edge[1:, :, REACH : 2 * REACH], edge[1:, :, 3 * REACH : 4 * REACH]], axis=1)
    image = got[:, :CELL_DEV, :]
    image += jnp.pad(after, ((1, 0), (0, 0), (0, outputs - REACH)))
    image += jnp.pad(before, ((0, 1), (0, 0), (outputs - REACH, 0)))
    return jnp.transpose(image, (1, 0, 2)).reshape(CELL_DEV, count * outputs)


def early_products(terms, pops, offsets):
    return pl.pallas_call(
        functools.partial(early_kernel, offsets=offsets),
        out_shape=jax.ShapeDtypeStruct((pops[0].shape[0], terms.shape[0]), F32),
        in_specs=[VMEM] * (1 + len(pops)),
        compiler_params=pltpu.CompilerParams(vmem_limit_bytes=VMEM_LIMIT),
        cost_estimate=pl.CostEstimate(flops=3 << 28, bytes_accessed=1 << 20, transcendentals=0),
        name="early",
    )(terms, *pops)


def slit_image(slit, terms, given, pops, offsets):
    cells, outputs = pops[0].shape[0], terms.shape[0] // 2 - 2 * REACH
    return pl.pallas_call(
        functools.partial(image_kernel, offsets=offsets),
        out_shape=jax.ShapeDtypeStruct((cells // CELL_DEV, CELL_DEV + 8, outputs), F32),
        in_specs=[SMEM] + [VMEM] * (2 + len(pops)),
        scratch_shapes=[pltpu.VMEM((cells + 16, outputs + 128), F32)],
        compiler_params=pltpu.CompilerParams(vmem_limit_bytes=VMEM_LIMIT),
        cost_estimate=pl.CostEstimate(flops=1 << 28, bytes_accessed=1 << 20, transcendentals=0),
        name="image",
    )(slit, terms, given, *pops)


def swap(values, offset, count):
    return lax.ppermute(values, "blk", [(i, i ^ offset) for i in range(count)])


def body(pop_cells, cell_map, line_level, line_strength, inst_wave, inst_slit):
    count = lax.axis_size("blk")
    own_levels = pop_cells.shape[0]
    bins = line_level.shape[0] // LINES_BIN
    outputs, chunks = bins // BINS, bins // CHUNK
    cells = CELL_DEV * count
    hold = lax.optimization_barrier

    onehot = (cell_map[None, :] == jnp.arange(cells, dtype=jnp.int32)[:, None]).astype(BF16)
    pop = lax.dot_general(onehot, pop_cells, CONTRACT_LAST, preferred_element_type=F32).astype(BF16)
    if count > HIGH:
        sets = [list(range(i, count, HIGH)) for i in range(HIGH)]
        pop = lax.all_gather(pop, "blk", axis=1, tiled=True, axis_index_groups=sets)

    lines = (line_level.reshape(-1, 128), line_strength.reshape(-1, 128), inst_wave.reshape(1, -1))
    far = [swap(pop, k, count) for k in (4, 8, 12)]
    total = emission_call(
        functools.partial(first_kernel, chunks=range(chunks // 2), own_levels=own_levels),
        jax.ShapeDtypeStruct((outputs + 2 * REACH, L), F32),
        lines,
        chunks // 2,
    )
    far, total = hold((far, total))
    line = jnp.concatenate([pop] + list(far), axis=1)
    across = swap(line, 2, count)
    line_pair = swap(line, 1, count)
    terms = emission_call(
        functools.partial(last_kernel, chunks=range(chunks // 2, chunks), own_levels=own_levels),
        jax.ShapeDtypeStruct((2 * outputs + 4 * REACH, L), BF16),
        lines + (total,),
        chunks - chunks // 2,
        [pltpu.VMEM((outputs + 2 * REACH, L), F32)],
    )
    across, terms = hold((across, terms))
    across_pair = swap(across, 1, count)
    offsets = [[k ^ offset for k in (0, 4, 8, 12)] for offset in (0, 1, 2, 3)]
    early = early_products(terms, [line, line_pair, across], offsets[:3])
    across_pair, early = hold((across_pair, early))
    image = slit_image(inst_slit, terms, early, [across_pair], offsets[3:])
    return join(lax.all_to_all(image, "blk", split_axis=0, concat_axis=0, tiled=True))


def solution(mesh):
    placed = (P("blk", "groups"), P(), P("blk"), P("blk"), P(), P())
    return jax.shard_map(
        body, mesh=mesh, in_specs=placed, out_specs=P(("groups", "blk"), None), check_vma=False
    )
```

```python
import functools

import jax
import jax.numpy as jnp
from jax import lax
from jax.experimental import pallas as pl
from jax.experimental.pallas import tpu as pltpu
from jax.sharding import PartitionSpec as P

L = 2048
LINES_BIN = 32
CELL_DEV = 16
LOW = 128
HIGH = L // LOW
BINS = 8
CHUNK = 256
REACH = 8
CHUNK_OUT = CHUNK // BINS
SPAN = CHUNK_OUT + 2 * REACH
CHUNK_ROWS = CHUNK * LINES_BIN // 128
TAP_WIDTH = 512
UNROLL = 4
BF16 = jnp.bfloat16
F32 = jnp.float32
VMEM_LIMIT = 48 * 1024 * 1024
CONTRACT_LAST = (((1,), (1,)), ((), ()))
VMEM = pl.BlockSpec(memory_space=pltpu.VMEM)
SMEM = pl.BlockSpec(memory_space=pltpu.SMEM)


def two_terms(values):
    first = values.astype(BF16)
    return first, (values - first.astype(F32)).astype(BF16)


def tap_matrix(wave_ref, tap_ref):
    tap_ref[...] = jnp.zeros_like(tap_ref)
    tap_ref[:, : wave_ref.shape[1]] = jnp.broadcast_to(wave_ref[...], (8, wave_ref.shape[1]))
    base = jnp.concatenate([tap_ref[...]] * (SPAN // 8), axis=0)
    taps = pltpu.roll(base, TAP_WIDTH - 128, 1, stride=BINS, stride_axis=0)[:, :CHUNK]
    return taps


def emission(lines, own_levels, scratch):
    level_ref, strength_ref, first_row, rows = lines
    high_ref, low_ref, em_ref = scratch
    level = level_ref[first_row : first_row + rows, :].astype(jnp.int32)
    owner = level // own_levels
    row_bin = lax.broadcasted_iota(jnp.int32, (rows, 128), 0) % 2 * (128 // LINES_BIN)
    lane_bin = lax.broadcasted_iota(jnp.int32, (rows, 128), 1) // LINES_BIN
    high_ref[:rows, :] = (owner % HIGH * BINS + row_bin + lane_bin).astype(F32)
    low_ref[:rows, :] = (owner // HIGH * own_levels + level % own_levels).astype(F32)

    choices = [
        (lax.broadcasted_iota(jnp.int32, (16, 128), 0) + 16 * block).astype(F32).astype(BF16)
        for block in range(LOW // 16)
    ]
    zero = jnp.zeros((16, 128), BF16)
    one = jnp.ones((16, 128), BF16)

    def spread(ref, index):
        return jnp.broadcast_to(ref[pl.ds(index, 1), :], (16, 128)).astype(BF16)

    def half(index):
        high = spread(high_ref, index)
        low = spread(low_ref, index)
        strength = spread(strength_ref, first_row + index)
        a = jnp.concatenate([jnp.where(high == choice, strength, zero) for choice in choices], axis=0)
        b = jnp.concatenate([jnp.where(low == choice, one, zero) for choice in choices], axis=0)
        return a, b

    def group(index):
        a0, b0 = half(2 * index)
        a1, b1 = half(2 * index + 1)
        return lax.dot_general(
            jnp.concatenate([a0, a1], axis=1),
            jnp.concatenate([b0, b1], axis=1),
            CONTRACT_LAST,
            preferred_element_type=F32,
        )

    @pl.loop(0, rows // 4, unroll=UNROLL)
    def _(pair):
        x = group(2 * pair)
        y = group(2 * pair + 1)
        place = pl.ds(pl.multiple_of(16 * pair, 16), 16)
        for h in range(HIGH):
            own = slice(BINS * h, BINS * h + BINS)
            em_ref[place, h * LOW : (h + 1) * LOW] = jnp.concatenate([x[own], y[own]], axis=0).astype(BF16)


def blurred(taps, em):
    rows = taps.shape[0]
    both = jnp.dot(jnp.concatenate(two_terms(taps), axis=0), em, preferred_element_type=F32)
    return both[:rows] + both[rows:]


def add_chunks(total_ref, chunks, taps, level_ref, strength_ref, own_levels, scratch):
    for chunk in chunks:
        emission((level_ref, strength_ref, chunk * CHUNK_ROWS, CHUNK_ROWS), own_levels, scratch)
        place = slice(chunk * CHUNK_OUT, chunk * CHUNK_OUT + SPAN)
        total_ref[place, :] += blurred(taps, scratch[-1][...])


def first_kernel(level_ref, strength_ref, wave_ref, total_ref, tap_ref, *scratch, chunks, own_levels):
    total_ref[...] = jnp.zeros_like(total_ref)
    taps = tap_matrix(wave_ref, tap_ref)
    add_chunks(total_ref, chunks, taps, level_ref, strength_ref, own_levels, scratch)


def last_kernel(
    level_ref, strength_ref, wave_ref, given_ref, out_ref, total_ref, tap_ref, *scratch, chunks, own_levels
):
    outputs = total_ref.shape[0] - 2 * REACH
    total_ref[...] = given_ref[...]
    taps = tap_matrix(wave_ref, tap_ref)
    add_chunks(total_ref, chunks, taps, level_ref, strength_ref, own_levels, scratch)
    first, second = two_terms(total_ref[REACH : REACH + outputs, :])
    out_ref[:outputs, :] = first
    out_ref[outputs : 2 * outputs, :] = second
    edges = jnp.concatenate([total_ref[REACH + outputs :, :], total_ref[:REACH, :]], axis=0)
    first, second = two_terms(edges)
    out_ref[2 * outputs : 2 * outputs + 2 * REACH, :] = first
    out_ref[2 * outputs + 2 * REACH :, :] = second


def emission_call(kernel, out_shape, operands, chunks, extra=()):
    scratch = [
        pltpu.VMEM((8, TAP_WIDTH), F32),
        pltpu.VMEM((CHUNK_ROWS, 128), F32),
        pltpu.VMEM((CHUNK_ROWS, 128), F32),
        pltpu.VMEM((CHUNK, L), BF16),
    ]
    return pl.pallas_call(
        kernel,
        out_shape=out_shape,
        in_specs=[VMEM] * len(operands),
        scratch_shapes=list(extra) + scratch,
        compiler_params=pltpu.CompilerParams(vmem_limit_bytes=VMEM_LIMIT),
        cost_estimate=pl.CostEstimate(
            flops=2 * chunks * CHUNK * L * 1024, bytes_accessed=chunks * CHUNK * 256, transcendentals=0
        ),
        name="emission",
    )(*operands)


def products(total, terms_ref, pop_refs, offsets):
    me = lax.axis_index("blk") % HIGH

    def block(offset):
        return terms_ref[:, pl.ds(pl.multiple_of((me ^ offset) * LOW, LOW), LOW)]

    for pop_ref, own in zip(pop_refs, offsets):
        for i in range(0, len(own), 2):
            terms = jnp.concatenate([block(own[i]), block(own[i + 1])], axis=1)
            pop = pop_ref[:, i * LOW : (i + 2) * LOW]
            new = lax.dot_general(pop, terms, CONTRACT_LAST, preferred_element_type=F32)
            total = new if total is None else total + new
    return total


def early_kernel(terms_ref, *refs, offsets):
    refs[-1][...] = products(None, terms_ref, refs[:-1], offsets)


def image_kernel(slit_ref, terms_ref, given_ref, *refs, offsets):
    pop_refs, (out_ref, pad_ref) = refs[:-2], refs[-2:]
    cells, outputs = pop_refs[0].shape[0], out_ref.shape[2]
    total = products(given_ref[...], terms_ref, pop_refs, offsets)
    edge = 2 * REACH
    pad_ref[:8, :] = jnp.zeros((8, pad_ref.shape[1]), F32)
    pad_ref[8 + cells :, :] = jnp.zeros((8, pad_ref.shape[1]), F32)
    pad_ref[8 : 8 + cells, :outputs] = total[:, :outputs] + total[:, outputs : 2 * outputs]
    pad_ref[8 : 8 + cells, outputs : outputs + edge] = (
        total[:, 2 * outputs : 2 * outputs + edge] + total[:, 2 * outputs + edge :]
    )
    image = slit_ref[0] * pad_ref[4 : 4 + cells, :]
    for tap in range(1, 9):
        image += slit_ref[tap] * pad_ref[4 + tap : 4 + tap + cells, :]
    lane = lax.broadcasted_iota(jnp.int32, (8, 128), 1)
    for place in range(cells // CELL_DEV):
        own = image[place * CELL_DEV : (place + 1) * CELL_DEV]
        out_ref[place, :CELL_DEV, :] = own[:, :outputs]
        moved = pltpu.roll(own[8:, outputs:], edge, 1)
        out_ref[place, CELL_DEV:, :] = jnp.where(lane < edge, own[:8, outputs:], moved)


def join(got):
    count, outputs = got.shape[0], got.shape[2]
    edge = got[:, CELL_DEV:, :]
    after = jnp.concatenate([edge[:-1, :, :REACH], edge[:-1, :, 2 * REACH : 3 * REACH]], axis=1)
    before = jnp.concatenate([edge[1:, :, REACH : 2 * REACH], edge[1:, :, 3 * REACH : 4 * REACH]], axis=1)
    image = got[:, :CELL_DEV, :]
    image += jnp.pad(after, ((1, 0), (0, 0), (0, outputs - REACH)))
    image += jnp.pad(before, ((0, 1), (0, 0), (outputs - REACH, 0)))
    return jnp.transpose(image, (1, 0, 2)).reshape(CELL_DEV, count * outputs)


def early_products(terms, pops, offsets):
    return pl.pallas_call(
        functools.partial(early_kernel, offsets=offsets),
        out_shape=jax.ShapeDtypeStruct((pops[0].shape[0], terms.shape[0]), F32),
        in_specs=[VMEM] * (1 + len(pops)),
        compiler_params=pltpu.CompilerParams(vmem_limit_bytes=VMEM_LIMIT),
        cost_estimate=pl.CostEstimate(flops=3 << 28, bytes_accessed=1 << 20, transcendentals=0),
        name="early",
    )(terms, *pops)


def slit_image(slit, terms, given, pops, offsets):
    cells, outputs = pops[0].shape[0], terms.shape[0] // 2 - 2 * REACH
    return pl.pallas_call(
        functools.partial(image_kernel, offsets=offsets),
        out_shape=jax.ShapeDtypeStruct((cells // CELL_DEV, CELL_DEV + 8, outputs), F32),
        in_specs=[SMEM] + [VMEM] * (2 + len(pops)),
        scratch_shapes=[pltpu.VMEM((cells + 16, outputs + 128), F32)],
        compiler_params=pltpu.CompilerParams(vmem_limit_bytes=VMEM_LIMIT),
        cost_estimate=pl.CostEstimate(flops=1 << 28, bytes_accessed=1 << 20, transcendentals=0),
        name="image",
    )(slit, terms, given, *pops)


def swap(values, offset, count):
    return lax.ppermute(values, "blk", [(i, i ^ offset) for i in range(count)])


def body(pop_cells, cell_map, line_level, line_strength, inst_wave, inst_slit):
    count = lax.axis_size("blk")
    own_levels = pop_cells.shape[0]
    bins = line_level.shape[0] // LINES_BIN
    outputs, chunks = bins // BINS, bins // CHUNK
    cells = CELL_DEV * count
    hold = lax.optimization_barrier

    onehot = (cell_map[None, :] == jnp.arange(cells, dtype=jnp.int32)[:, None]).astype(BF16)
    pop = lax.dot_general(onehot, pop_cells, CONTRACT_LAST, preferred_element_type=F32).astype(BF16)
    if count > HIGH:
        sets = [list(range(i, count, HIGH)) for i in range(HIGH)]
        pop = lax.all_gather(pop, "blk", axis=1, tiled=True, axis_index_groups=sets)

    lines = (line_level.reshape(-1, 128), line_strength.reshape(-1, 128), inst_wave.reshape(1, -1))
    early = chunks // 4
    far = [swap(pop, k, count) for k in (4, 8, 12)]
    total = emission_call(
        functools.partial(first_kernel, chunks=range(early), own_levels=own_levels),
        jax.ShapeDtypeStruct((outputs + 2 * REACH, L), F32),
        lines,
        early,
    )
    far, total = hold((far, total))
    line = jnp.concatenate([pop] + list(far), axis=1)
    across = swap(line, 2, count)
    line_pair = swap(line, 1, count)
    terms = emission_call(
        functools.partial(last_kernel, chunks=range(early, chunks), own_levels=own_levels),
        jax.ShapeDtypeStruct((2 * outputs + 4 * REACH, L), BF16),
        lines + (total,),
        chunks - early,
        [pltpu.VMEM((outputs + 2 * REACH, L), F32)],
    )
    across, terms = hold((across, terms))
    across_pair = swap(across, 1, count)
    offsets = [[k ^ offset for k in (0, 4, 8, 12)] for offset in (0, 1, 2, 3)]
    near = early_products(terms, [line, line_pair, across], offsets[:3])
    across_pair, near = hold((across_pair, near))
    image = slit_image(inst_slit, terms, near, [across_pair], offsets[3:])
    return join(lax.all_to_all(image, "blk", split_axis=0, concat_axis=0, tiled=True))


def solution(mesh):
    placed = (P("blk", "groups"), P(), P("blk"), P("blk"), P(), P())
    return jax.shard_map(
        body, mesh=mesh, in_specs=placed, out_specs=P(("groups", "blk"), None), check_vma=False
    )
```

```python
import functools

import jax
import jax.numpy as jnp
from jax import lax
from jax.experimental import pallas as pl
from jax.experimental.pallas import tpu as pltpu
from jax.sharding import PartitionSpec as P

L = 2048
LINES_BIN = 32
CELL_DEV = 16
LOW = 128
HIGH = L // LOW
BINS = 8
CHUNK = 256
REACH = 8
CHUNK_OUT = CHUNK // BINS
SPAN = CHUNK_OUT + 2 * REACH
CHUNK_ROWS = CHUNK * LINES_BIN // 128
TAP_WIDTH = 512
UNROLL = 16
BF16 = jnp.bfloat16
F32 = jnp.float32
VMEM_LIMIT = 48 * 1024 * 1024
CONTRACT_LAST = (((1,), (1,)), ((), ()))
VMEM = pl.BlockSpec(memory_space=pltpu.VMEM)
SMEM = pl.BlockSpec(memory_space=pltpu.SMEM)


def two_terms(values):
    first = values.astype(BF16)
    return first, (values - first.astype(F32)).astype(BF16)


def tap_matrix(wave_ref, tap_ref):
    tap_ref[...] = jnp.zeros_like(tap_ref)
    tap_ref[:, : wave_ref.shape[1]] = jnp.broadcast_to(wave_ref[...], (8, wave_ref.shape[1]))
    base = jnp.concatenate([tap_ref[...]] * (SPAN // 8), axis=0)
    taps = pltpu.roll(base, TAP_WIDTH - 128, 1, stride=BINS, stride_axis=0)[:, :CHUNK]
    return taps


def emission(lines, own_levels, scratch):
    level_ref, strength_ref, first_row, rows = lines
    high_ref, low_ref, em_ref = scratch
    level = level_ref[first_row : first_row + rows, :].astype(jnp.int32)
    owner = level // own_levels
    row_bin = lax.broadcasted_iota(jnp.int32, (rows, 128), 0) % 2 * (128 // LINES_BIN)
    lane_bin = lax.broadcasted_iota(jnp.int32, (rows, 128), 1) // LINES_BIN
    high_ref[:rows, :] = (owner % HIGH * BINS + row_bin + lane_bin).astype(F32)
    low_ref[:rows, :] = (owner // HIGH * own_levels + level % own_levels).astype(F32)

    choices = [
        (lax.broadcasted_iota(jnp.int32, (16, 128), 0) + 16 * block).astype(F32).astype(BF16)
        for block in range(LOW // 16)
    ]
    zero = jnp.zeros((16, 128), BF16)
    one = jnp.ones((16, 128), BF16)

    def spread(ref, index):
        return jnp.broadcast_to(ref[pl.ds(index, 1), :], (16, 128)).astype(BF16)

    def half(index):
        high = spread(high_ref, index)
        low = spread(low_ref, index)
        strength = spread(strength_ref, first_row + index)
        a = jnp.concatenate([jnp.where(high == choice, strength, zero) for choice in choices], axis=0)
        b = jnp.concatenate([jnp.where(low == choice, one, zero) for choice in choices], axis=0)
        return a, b

    def group(index):
        a0, b0 = half(2 * index)
        a1, b1 = half(2 * index + 1)
        return lax.dot_general(
            jnp.concatenate([a0, a1], axis=1),
            jnp.concatenate([b0, b1], axis=1),
            CONTRACT_LAST,
            preferred_element_type=F32,
        )

    @pl.loop(0, rows // 4, unroll=UNROLL)
    def _(pair):
        x = group(2 * pair)
        y = group(2 * pair + 1)
        place = pl.ds(pl.multiple_of(16 * pair, 16), 16)
        for h in range(HIGH):
            own = slice(BINS * h, BINS * h + BINS)
            em_ref[place, h * LOW : (h + 1) * LOW] = jnp.concatenate([x[own], y[own]], axis=0).astype(BF16)


def blurred(taps, em):
    rows = taps.shape[0]
    both = jnp.dot(jnp.concatenate(two_terms(taps), axis=0), em, preferred_element_type=F32)
    return both[:rows] + both[rows:]


def add_chunks(total_ref, chunks, taps, level_ref, strength_ref, own_levels, scratch):
    for chunk in chunks:
        emission((level_ref, strength_ref, chunk * CHUNK_ROWS, CHUNK_ROWS), own_levels, scratch)
        place = slice(chunk * CHUNK_OUT, chunk * CHUNK_OUT + SPAN)
        total_ref[place, :] += blurred(taps, scratch[-1][...])


def first_kernel(level_ref, strength_ref, wave_ref, total_ref, tap_ref, *scratch, chunks, own_levels):
    total_ref[...] = jnp.zeros_like(total_ref)
    taps = tap_matrix(wave_ref, tap_ref)
    add_chunks(total_ref, chunks, taps, level_ref, strength_ref, own_levels, scratch)


def last_kernel(
    level_ref, strength_ref, wave_ref, given_ref, out_ref, total_ref, tap_ref, *scratch, chunks, own_levels
):
    outputs = total_ref.shape[0] - 2 * REACH
    total_ref[...] = given_ref[...]
    taps = tap_matrix(wave_ref, tap_ref)
    add_chunks(total_ref, chunks, taps, level_ref, strength_ref, own_levels, scratch)
    first, second = two_terms(total_ref[REACH : REACH + outputs, :])
    out_ref[:outputs, :] = first
    out_ref[outputs : 2 * outputs, :] = second
    edges = jnp.concatenate([total_ref[REACH + outputs :, :], total_ref[:REACH, :]], axis=0)
    first, second = two_terms(edges)
    out_ref[2 * outputs : 2 * outputs + 2 * REACH, :] = first
    out_ref[2 * outputs + 2 * REACH :, :] = second


def emission_call(kernel, out_shape, operands, chunks, extra=()):
    scratch = [
        pltpu.VMEM((8, TAP_WIDTH), F32),
        pltpu.VMEM((CHUNK_ROWS, 128), F32),
        pltpu.VMEM((CHUNK_ROWS, 128), F32),
        pltpu.VMEM((CHUNK, L), BF16),
    ]
    return pl.pallas_call(
        kernel,
        out_shape=out_shape,
        in_specs=[VMEM] * len(operands),
        scratch_shapes=list(extra) + scratch,
        compiler_params=pltpu.CompilerParams(vmem_limit_bytes=VMEM_LIMIT),
        cost_estimate=pl.CostEstimate(
            flops=2 * chunks * CHUNK * L * 1024, bytes_accessed=chunks * CHUNK * 256, transcendentals=0
        ),
        name="emission",
    )(*operands)


def products(total, terms_ref, pop_refs, offsets):
    me = lax.axis_index("blk") % HIGH

    def block(offset):
        return terms_ref[:, pl.ds(pl.multiple_of((me ^ offset) * LOW, LOW), LOW)]

    for pop_ref, own in zip(pop_refs, offsets):
        for i in range(0, len(own), 2):
            terms = jnp.concatenate([block(offset) for offset in own[i : i + 2]], axis=1)
            pop = pop_ref[:, i * LOW : i * LOW + terms.shape[1]]
            new = lax.dot_general(pop, terms, CONTRACT_LAST, preferred_element_type=F32)
            total = new if total is None else total + new
    return total


def early_kernel(terms_ref, *refs, offsets):
    refs[-1][...] = products(None, terms_ref, refs[:-1], offsets)


def image_kernel(slit_ref, terms_ref, given_ref, *refs, offsets):
    pop_refs, (out_ref, pad_ref) = refs[:-2], refs[-2:]
    cells, outputs = pop_refs[0].shape[0], out_ref.shape[2]
    total = products(given_ref[...], terms_ref, pop_refs, offsets)
    edge = 2 * REACH
    pad_ref[:8, :] = jnp.zeros((8, pad_ref.shape[1]), F32)
    pad_ref[8 + cells :, :] = jnp.zeros((8, pad_ref.shape[1]), F32)
    pad_ref[8 : 8 + cells, :outputs] = total[:, :outputs] + total[:, outputs : 2 * outputs]
    pad_ref[8 : 8 + cells, outputs : outputs + edge] = (
        total[:, 2 * outputs : 2 * outputs + edge] + total[:, 2 * outputs + edge :]
    )
    image = slit_ref[0] * pad_ref[4 : 4 + cells, :]
    for tap in range(1, 9):
        image += slit_ref[tap] * pad_ref[4 + tap : 4 + tap + cells, :]
    lane = lax.broadcasted_iota(jnp.int32, (8, 128), 1)
    for place in range(cells // CELL_DEV):
        own = image[place * CELL_DEV : (place + 1) * CELL_DEV]
        out_ref[place, :CELL_DEV, :] = own[:, :outputs]
        moved = pltpu.roll(own[8:, outputs:], edge, 1)
        out_ref[place, CELL_DEV:, :] = jnp.where(lane < edge, own[:8, outputs:], moved)


def join(got):
    count, outputs = got.shape[0], got.shape[2]
    edge = got[:, CELL_DEV:, :]
    after = jnp.concatenate([edge[:-1, :, :REACH], edge[:-1, :, 2 * REACH : 3 * REACH]], axis=1)
    before = jnp.concatenate([edge[1:, :, REACH : 2 * REACH], edge[1:, :, 3 * REACH : 4 * REACH]], axis=1)
    image = got[:, :CELL_DEV, :]
    image += jnp.pad(after, ((1, 0), (0, 0), (0, outputs - REACH)))
    image += jnp.pad(before, ((0, 1), (0, 0), (outputs - REACH, 0)))
    return jnp.transpose(image, (1, 0, 2)).reshape(CELL_DEV, count * outputs)


def early_products(terms, pops, offsets):
    return pl.pallas_call(
        functools.partial(early_kernel, offsets=offsets),
        out_shape=jax.ShapeDtypeStruct((pops[0].shape[0], terms.shape[0]), F32),
        in_specs=[VMEM] * (1 + len(pops)),
        compiler_params=pltpu.CompilerParams(vmem_limit_bytes=VMEM_LIMIT),
        cost_estimate=pl.CostEstimate(flops=3 << 28, bytes_accessed=1 << 20, transcendentals=0),
        name="early",
    )(terms, *pops)


def slit_image(slit, terms, given, pops, offsets):
    cells, outputs = pops[0].shape[0], terms.shape[0] // 2 - 2 * REACH
    return pl.pallas_call(
        functools.partial(image_kernel, offsets=offsets),
        out_shape=jax.ShapeDtypeStruct((cells // CELL_DEV, CELL_DEV + 8, outputs), F32),
        in_specs=[SMEM] + [VMEM] * (2 + len(pops)),
        scratch_shapes=[pltpu.VMEM((cells + 16, outputs + 128), F32)],
        compiler_params=pltpu.CompilerParams(vmem_limit_bytes=VMEM_LIMIT),
        cost_estimate=pl.CostEstimate(flops=1 << 28, bytes_accessed=1 << 20, transcendentals=0),
        name="image",
    )(slit, terms, given, *pops)


def swap(values, offset, count):
    return lax.ppermute(values, "blk", [(i, i ^ offset) for i in range(count)])


def body(pop_cells, cell_map, line_level, line_strength, inst_wave, inst_slit):
    count = lax.axis_size("blk")
    own_levels = pop_cells.shape[0]
    bins = line_level.shape[0] // LINES_BIN
    outputs, chunks = bins // BINS, bins // CHUNK
    cells = CELL_DEV * count
    hold = lax.optimization_barrier

    onehot = (cell_map[None, :] == jnp.arange(cells, dtype=jnp.int32)[:, None]).astype(BF16)
    pop = lax.dot_general(onehot, pop_cells, CONTRACT_LAST, preferred_element_type=F32).astype(BF16)
    if count > HIGH:
        sets = [list(range(i, count, HIGH)) for i in range(HIGH)]
        pop = lax.all_gather(pop, "blk", axis=1, tiled=True, axis_index_groups=sets)

    lines = (line_level.reshape(-1, 128), line_strength.reshape(-1, 128), inst_wave.reshape(1, -1))
    early = chunks // 4
    far = [swap(pop, k, count) for k in (4, 8, 12)]
    beside = swap(pop, 2, count)
    total = emission_call(
        functools.partial(first_kernel, chunks=range(early), own_levels=own_levels),
        jax.ShapeDtypeStruct((outputs + 2 * REACH, L), F32),
        lines,
        early,
    )
    far, beside, total = hold((far, beside, total))
    line = jnp.concatenate(list(far), axis=1)
    across = swap(line, 2, count)
    near = jnp.concatenate([pop, beside], axis=1)
    line_pair, near_pair = swap(line, 1, count), swap(near, 1, count)
    terms = emission_call(
        functools.partial(last_kernel, chunks=range(early, chunks), own_levels=own_levels),
        jax.ShapeDtypeStruct((2 * outputs + 4 * REACH, L), BF16),
        lines + (total,),
        chunks - early,
        [pltpu.VMEM((outputs + 2 * REACH, L), F32)],
    )
    across, terms = hold((across, terms))
    across_pair = swap(across, 1, count)
    z = [4, 8, 12]
    first = early_products(
        terms,
        [near, line, line_pair, near_pair, across],
        [[0, 2], z, [k ^ 1 for k in z], [1, 3], [k ^ 2 for k in z]],
    )
    across_pair, first = hold((across_pair, first))
    image = slit_image(inst_slit, terms, first, [across_pair], [[k ^ 3 for k in z]])
    return join(lax.all_to_all(image, "blk", split_axis=0, concat_axis=0, tiled=True))


def solution(mesh):
    placed = (P("blk", "groups"), P(), P("blk"), P("blk"), P(), P())
    return jax.shard_map(
        body, mesh=mesh, in_specs=placed, out_specs=P(("groups", "blk"), None), check_vma=False
    )
```

```python
import functools

import jax
import jax.numpy as jnp
from jax import lax
from jax.experimental import pallas as pl
from jax.experimental.pallas import tpu as pltpu
from jax.sharding import PartitionSpec as P

L = 2048
LINES_BIN = 32
CELL_DEV = 16
LOW = 128
HIGH = L // LOW
BINS = 8
CHUNK = 256
REACH = 8
CHUNK_OUT = CHUNK // BINS
SPAN = CHUNK_OUT + 2 * REACH
CHUNK_ROWS = CHUNK * LINES_BIN // 128
TAP_WIDTH = 512
TAP_FLOPS = 1 << 32
UNROLL = 16
EARLY = 1
BF16 = jnp.bfloat16
F32 = jnp.float32
VMEM_LIMIT = 48 * 1024 * 1024
CONTRACT_LAST = (((1,), (1,)), ((), ()))
VMEM = pl.BlockSpec(memory_space=pltpu.VMEM)


def two_terms(values):
    first = values.astype(BF16)
    return first, (values - first.astype(F32)).astype(BF16)


def tap_kernel(wave_ref, out_ref, tap_ref):
    tap_ref[...] = jnp.zeros_like(tap_ref)
    tap_ref[:, : wave_ref.shape[1]] = jnp.broadcast_to(wave_ref[...], (8, wave_ref.shape[1]))
    base = jnp.concatenate([tap_ref[...]] * (SPAN // 8), axis=0)
    taps = pltpu.roll(base, TAP_WIDTH - 128, 1, stride=BINS, stride_axis=0)[:, :CHUNK]
    first, second = two_terms(taps)
    out_ref[:SPAN, :] = first
    out_ref[SPAN:, :] = second


def tap_matrix(wave):
    return pl.pallas_call(
        tap_kernel,
        out_shape=jax.ShapeDtypeStruct((2 * SPAN, CHUNK), BF16),
        in_specs=[VMEM],
        scratch_shapes=[pltpu.VMEM((8, TAP_WIDTH), F32)],
        cost_estimate=pl.CostEstimate(flops=TAP_FLOPS, bytes_accessed=1 << 16, transcendentals=0),
        name="taps",
    )(wave)


def emission(lines, own_levels, scratch):
    level_ref, strength_ref, first_row, rows = lines
    high_ref, low_ref, em_ref = scratch
    level = level_ref[first_row : first_row + rows, :].astype(jnp.int32)
    owner = level // own_levels
    row_bin = lax.broadcasted_iota(jnp.int32, (rows, 128), 0) % 2 * (128 // LINES_BIN)
    lane_bin = lax.broadcasted_iota(jnp.int32, (rows, 128), 1) // LINES_BIN
    high_ref[:rows, :] = (owner % HIGH * BINS + row_bin + lane_bin).astype(F32)
    low_ref[:rows, :] = (owner // HIGH * own_levels + level % own_levels).astype(F32)

    choices = [
        (lax.broadcasted_iota(jnp.int32, (16, 128), 0) + 16 * block).astype(F32).astype(BF16)
        for block in range(LOW // 16)
    ]
    zero = jnp.zeros((16, 128), BF16)
    one = jnp.ones((16, 128), BF16)

    def spread(ref, index):
        return jnp.broadcast_to(ref[pl.ds(index, 1), :], (16, 128)).astype(BF16)

    def half(index):
        high = spread(high_ref, index)
        low = spread(low_ref, index)
        strength = spread(strength_ref, first_row + index)
        a = jnp.concatenate([jnp.where(high == choice, strength, zero) for choice in choices], axis=0)
        b = jnp.concatenate([jnp.where(low == choice, one, zero) for choice in choices], axis=0)
        return a, b

    def group(index):
        a0, b0 = half(2 * index)
        a1, b1 = half(2 * index + 1)
        return lax.dot_general(
            jnp.concatenate([a0, a1], axis=1),
            jnp.concatenate([b0, b1], axis=1),
            CONTRACT_LAST,
            preferred_element_type=F32,
        )

    @pl.loop(0, rows // 4, unroll=UNROLL)
    def _(pair):
        x = group(2 * pair)
        y = group(2 * pair + 1)
        place = pl.ds(pl.multiple_of(16 * pair, 16), 16)
        for h in range(HIGH):
            own = slice(BINS * h, BINS * h + BINS)
            em_ref[place, h * LOW : (h + 1) * LOW] = jnp.concatenate([x[own], y[own]], axis=0).astype(BF16)


def blurred(taps, em):
    both = jnp.dot(taps, em, preferred_element_type=F32)
    return both[:SPAN] + both[SPAN:]


def add_chunks(total_ref, chunks, taps, level_ref, strength_ref, own_levels, scratch):
    for chunk in chunks:
        emission((level_ref, strength_ref, chunk * CHUNK_ROWS, CHUNK_ROWS), own_levels, scratch)
        place = slice(chunk * CHUNK_OUT, chunk * CHUNK_OUT + SPAN)
        total_ref[place, :] += blurred(taps, scratch[-1][...])


def first_kernel(level_ref, strength_ref, taps_ref, total_ref, *scratch, chunks, own_levels):
    total_ref[...] = jnp.zeros_like(total_ref)
    add_chunks(total_ref, chunks, taps_ref[...], level_ref, strength_ref, own_levels, scratch)


def last_kernel(
    level_ref, strength_ref, taps_ref, given_ref, out_ref, total_ref, *scratch, chunks, own_levels
):
    outputs = total_ref.shape[0] - 2 * REACH
    total_ref[...] = given_ref[...]
    add_chunks(total_ref, chunks, taps_ref[...], level_ref, strength_ref, own_levels, scratch)
    first, second = two_terms(total_ref[REACH : REACH + outputs, :])
    out_ref[:outputs, :] = first
    out_ref[outputs : 2 * outputs, :] = second
    edges = jnp.concatenate([total_ref[REACH + outputs :, :], total_ref[:REACH, :]], axis=0)
    first, second = two_terms(edges)
    out_ref[2 * outputs : 2 * outputs + 2 * REACH, :] = first
    out_ref[2 * outputs + 2 * REACH :, :] = second


def emission_call(kernel, out_shape, operands, chunks, extra=()):
    scratch = [
        pltpu.VMEM((CHUNK_ROWS, 128), F32),
        pltpu.VMEM((CHUNK_ROWS, 128), F32),
        pltpu.VMEM((CHUNK, L), BF16),
    ]
    return pl.pallas_call(
        kernel,
        out_shape=out_shape,
        in_specs=[VMEM] * len(operands),
        scratch_shapes=list(extra) + scratch,
        compiler_params=pltpu.CompilerParams(vmem_limit_bytes=VMEM_LIMIT),
        cost_estimate=pl.CostEstimate(
            flops=2 * chunks * CHUNK * L * 32, bytes_accessed=chunks * CHUNK * 256, transcendentals=0
        ),
        name="emission",
    )(*operands)


def products(total, terms_ref, pop_refs, offsets):
    me = lax.axis_index("blk") % HIGH

    def block(offset):
        return terms_ref[:, pl.ds(pl.multiple_of((me ^ offset) * LOW, LOW), LOW)]

    for pop_ref, own in zip(pop_refs, offsets):
        for i in range(0, len(own), 2):
            terms = jnp.concatenate([block(offset) for offset in own[i : i + 2]], axis=1)
            pop = pop_ref[:, i * LOW : i * LOW + terms.shape[1]]
            new = lax.dot_general(pop, terms, CONTRACT_LAST, preferred_element_type=F32)
            total = new if total is None else total + new
    return total


def early_kernel(terms_ref, *refs, offsets):
    refs[-1][...] = products(None, terms_ref, refs[:-1], offsets)


def image_kernel(slit_ref, terms_ref, given_ref, *refs, offsets):
    pop_refs, (out_ref, pad_ref) = refs[:-2], refs[-2:]
    cells, outputs = pop_refs[0].shape[0], out_ref.shape[2]
    total = products(given_ref[...], terms_ref, pop_refs, offsets)
    edge = 2 * REACH
    pad_ref[:8, :] = jnp.zeros((8, pad_ref.shape[1]), F32)
    pad_ref[8 + cells :, :] = jnp.zeros((8, pad_ref.shape[1]), F32)
    pad_ref[8 : 8 + cells, :outputs] = total[:, :outputs] + total[:, outputs : 2 * outputs]
    pad_ref[8 : 8 + cells, outputs : outputs + edge] = (
        total[:, 2 * outputs : 2 * outputs + edge] + total[:, 2 * outputs + edge :]
    )
    image = slit_ref[:, 0:1] * pad_ref[4 : 4 + cells, :]
    for tap in range(1, 9):
        image += slit_ref[:, tap : tap + 1] * pad_ref[4 + tap : 4 + tap + cells, :]
    lane = lax.broadcasted_iota(jnp.int32, (8, 128), 1)
    for place in range(cells // CELL_DEV):
        own = image[place * CELL_DEV : (place + 1) * CELL_DEV]
        out_ref[place, :CELL_DEV, :] = own[:, :outputs]
        moved = pltpu.roll(own[8:, outputs:], edge, 1)
        out_ref[place, CELL_DEV:, :] = jnp.where(lane < edge, own[:8, outputs:], moved)


def join(got):
    count, outputs = got.shape[0], got.shape[2]
    edge = got[:, CELL_DEV:, :]
    after = jnp.concatenate([edge[:-1, :, :REACH], edge[:-1, :, 2 * REACH : 3 * REACH]], axis=1)
    before = jnp.concatenate([edge[1:, :, REACH : 2 * REACH], edge[1:, :, 3 * REACH : 4 * REACH]], axis=1)
    image = got[:, :CELL_DEV, :]
    image += jnp.pad(after, ((1, 0), (0, 0), (0, outputs - REACH)))
    image += jnp.pad(before, ((0, 1), (0, 0), (outputs - REACH, 0)))
    return jnp.transpose(image, (1, 0, 2)).reshape(CELL_DEV, count * outputs)


def early_products(terms, pops, offsets):
    return pl.pallas_call(
        functools.partial(early_kernel, offsets=offsets),
        out_shape=jax.ShapeDtypeStruct((pops[0].shape[0], terms.shape[0]), F32),
        in_specs=[VMEM] * (1 + len(pops)),
        compiler_params=pltpu.CompilerParams(vmem_limit_bytes=VMEM_LIMIT),
        cost_estimate=pl.CostEstimate(flops=3 << 28, bytes_accessed=1 << 20, transcendentals=0),
        name="early",
    )(terms, *pops)


def slit_image(slit, terms, given, pops, offsets):
    cells, outputs = pops[0].shape[0], terms.shape[0] // 2 - 2 * REACH
    return pl.pallas_call(
        functools.partial(image_kernel, offsets=offsets),
        out_shape=jax.ShapeDtypeStruct((cells // CELL_DEV, CELL_DEV + 8, outputs), F32),
        in_specs=[VMEM] * (3 + len(pops)),
        scratch_shapes=[pltpu.VMEM((cells + 16, outputs + 128), F32)],
        compiler_params=pltpu.CompilerParams(vmem_limit_bytes=VMEM_LIMIT),
        cost_estimate=pl.CostEstimate(flops=1 << 28, bytes_accessed=1 << 20, transcendentals=0),
        name="image",
    )(slit, terms, given, *pops)


def swap(values, offset, count):
    return lax.ppermute(values, "blk", [(i, i ^ offset) for i in range(count)])


def body(pop_cells, cell_map, line_level, line_strength, inst_wave, inst_slit):
    count = lax.axis_size("blk")
    own_levels = pop_cells.shape[0]
    bins = line_level.shape[0] // LINES_BIN
    outputs, chunks = bins // BINS, bins // CHUNK
    cells = CELL_DEV * count
    hold = lax.optimization_barrier

    onehot = (cell_map[None, :] == jnp.arange(cells, dtype=jnp.int32)[:, None]).astype(BF16)
    pop = lax.dot_general(onehot, pop_cells, CONTRACT_LAST, preferred_element_type=F32).astype(BF16)
    if count > HIGH:
        sets = [list(range(i, count, HIGH)) for i in range(HIGH)]
        pop = lax.all_gather(pop, "blk", axis=1, tiled=True, axis_index_groups=sets)

    lines = (line_level.reshape(-1, 128), line_strength.reshape(-1, 128), tap_matrix(inst_wave.reshape(1, -1)))
    early = EARLY
    far = [swap(pop, k, count) for k in (4, 8, 12)]
    beside = swap(pop, 2, count)
    total = emission_call(
        functools.partial(first_kernel, chunks=range(early), own_levels=own_levels),
        jax.ShapeDtypeStruct((outputs + 2 * REACH, L), F32),
        lines,
        early,
    )
    far, beside, total = hold((far, beside, total))
    pair, beside = hold((jnp.concatenate(far[1:], axis=1), beside))
    across = swap(pair, 2, count)
    corner = swap(beside, 4, count)
    near = jnp.concatenate([pop, beside] + list(far), axis=1)
    near_pair = swap(near, 1, count)
    terms = emission_call(
        functools.partial(last_kernel, chunks=range(early, chunks), own_levels=own_levels),
        jax.ShapeDtypeStruct((2 * outputs + 4 * REACH, L), BF16),
        lines + (total,),
        chunks - early,
        [pltpu.VMEM((outputs + 2 * REACH, L), F32)],
    )
    across, corner, terms = hold((across, corner, terms))
    rest = jnp.concatenate([across, corner], axis=1)
    rest_pair = swap(rest, 1, count)
    first = early_products(terms, [near, near_pair, rest], [[0, 2, 4, 8, 12], [1, 3, 5, 9, 13], [10, 14, 6]])
    rest_pair, first = hold((rest_pair, first))
    image = slit_image(inst_slit.reshape(1, -1), terms, first, [rest_pair], [[11, 15, 7]])
    return join(lax.all_to_all(image, "blk", split_axis=0, concat_axis=0, tiled=True))


def solution(mesh):
    placed = (P("blk", "groups"), P(), P("blk"), P("blk"), P(), P())
    return jax.shard_map(
        body, mesh=mesh, in_specs=placed, out_specs=P(("groups", "blk"), None), check_vma=False
    )
```

```python
import functools

import jax
import jax.numpy as jnp
from jax import lax
from jax.experimental import pallas as pl
from jax.experimental.pallas import tpu as pltpu
from jax.sharding import PartitionSpec as P

L = 2048
LINES_BIN = 32
CELL_DEV = 16
LOW = 128
HIGH = L // LOW
BINS = 8
CHUNK = 256
REACH = 8
CHUNK_OUT = CHUNK // BINS
SPAN = CHUNK_OUT + 2 * REACH
CHUNK_ROWS = CHUNK * LINES_BIN // 128
TAP_WIDTH = 512
TAP_FLOPS = 1 << 32
UNROLL = 16
EARLY = 1
BF16 = jnp.bfloat16
F32 = jnp.float32
VMEM_LIMIT = 48 * 1024 * 1024
CONTRACT_LAST = (((1,), (1,)), ((), ()))
VMEM = pl.BlockSpec(memory_space=pltpu.VMEM)


def two_terms(values):
    first = values.astype(BF16)
    return first, (values - first.astype(F32)).astype(BF16)


def tap_kernel(wave_ref, out_ref, tap_ref):
    tap_ref[...] = jnp.zeros_like(tap_ref)
    tap_ref[:, : wave_ref.shape[1]] = jnp.broadcast_to(wave_ref[...], (8, wave_ref.shape[1]))
    base = jnp.concatenate([tap_ref[...]] * (SPAN // 8), axis=0)
    taps = pltpu.roll(base, TAP_WIDTH - 128, 1, stride=BINS, stride_axis=0)[:, :CHUNK]
    first, second = two_terms(taps)
    out_ref[:SPAN, :] = first
    out_ref[SPAN:, :] = second


def tap_matrix(wave):
    return pl.pallas_call(
        tap_kernel,
        out_shape=jax.ShapeDtypeStruct((2 * SPAN, CHUNK), BF16),
        in_specs=[VMEM],
        scratch_shapes=[pltpu.VMEM((8, TAP_WIDTH), F32)],
        compiler_params=pltpu.CompilerParams(vmem_limit_bytes=VMEM_LIMIT),
        cost_estimate=pl.CostEstimate(flops=TAP_FLOPS, bytes_accessed=1 << 16, transcendentals=0),
        name="taps",
    )(wave)


def emission(lines, own_levels, scratch):
    level_ref, strength_ref, first_row, rows = lines
    high_ref, low_ref, em_ref = scratch
    level = level_ref[first_row : first_row + rows, :].astype(jnp.int32)
    owner = level // own_levels
    row_bin = lax.broadcasted_iota(jnp.int32, (rows, 128), 0) % 2 * (128 // LINES_BIN)
    lane_bin = lax.broadcasted_iota(jnp.int32, (rows, 128), 1) // LINES_BIN
    high_ref[:rows, :] = (owner % HIGH * BINS + row_bin + lane_bin).astype(F32)
    low_ref[:rows, :] = (owner // HIGH * own_levels + level % own_levels).astype(F32)

    choices = [
        (lax.broadcasted_iota(jnp.int32, (16, 128), 0) + 16 * block).astype(F32).astype(BF16)
        for block in range(LOW // 16)
    ]
    zero = jnp.zeros((16, 128), BF16)
    one = jnp.ones((16, 128), BF16)

    def spread(ref, index):
        return jnp.broadcast_to(ref[pl.ds(index, 1), :], (16, 128)).astype(BF16)

    def half(index):
        high = spread(high_ref, index)
        low = spread(low_ref, index)
        strength = spread(strength_ref, first_row + index)
        a = jnp.concatenate([jnp.where(high == choice, strength, zero) for choice in choices], axis=0)
        b = jnp.concatenate([jnp.where(low == choice, one, zero) for choice in choices], axis=0)
        return a, b

    def group(index):
        a0, b0 = half(2 * index)
        a1, b1 = half(2 * index + 1)
        return lax.dot_general(
            jnp.concatenate([a0, a1], axis=1),
            jnp.concatenate([b0, b1], axis=1),
            CONTRACT_LAST,
            preferred_element_type=F32,
        )

    @pl.loop(0, rows // 4, unroll=UNROLL)
    def _(pair):
        x = group(2 * pair)
        y = group(2 * pair + 1)
        place = pl.ds(pl.multiple_of(16 * pair, 16), 16)
        for h in range(HIGH):
            own = slice(BINS * h, BINS * h + BINS)
            em_ref[place, h * LOW : (h + 1) * LOW] = jnp.concatenate([x[own], y[own]], axis=0).astype(BF16)


def blurred(taps, em):
    both = jnp.dot(taps, em, preferred_element_type=F32)
    return both[:SPAN] + both[SPAN:]


def add_chunks(total_ref, chunks, taps, level_ref, strength_ref, own_levels, scratch):
    for chunk in chunks:
        emission((level_ref, strength_ref, chunk * CHUNK_ROWS, CHUNK_ROWS), own_levels, scratch)
        place = slice(chunk * CHUNK_OUT, chunk * CHUNK_OUT + SPAN)
        total_ref[place, :] += blurred(taps, scratch[-1][...])


def first_kernel(level_ref, strength_ref, taps_ref, total_ref, *scratch, chunks, own_levels):
    total_ref[...] = jnp.zeros_like(total_ref)
    add_chunks(total_ref, chunks, taps_ref[...], level_ref, strength_ref, own_levels, scratch)


def last_kernel(
    level_ref, strength_ref, taps_ref, given_ref, out_ref, total_ref, *scratch, chunks, own_levels
):
    outputs = total_ref.shape[0] - 2 * REACH
    total_ref[...] = given_ref[...]
    add_chunks(total_ref, chunks, taps_ref[...], level_ref, strength_ref, own_levels, scratch)
    first, second = two_terms(total_ref[REACH : REACH + outputs, :])
    out_ref[:outputs, :] = first
    out_ref[outputs : 2 * outputs, :] = second
    edges = jnp.concatenate([total_ref[REACH + outputs :, :], total_ref[:REACH, :]], axis=0)
    first, second = two_terms(edges)
    out_ref[2 * outputs : 2 * outputs + 2 * REACH, :] = first
    out_ref[2 * outputs + 2 * REACH :, :] = second


def emission_call(kernel, out_shape, operands, chunks, extra=()):
    scratch = [
        pltpu.VMEM((CHUNK_ROWS, 128), F32),
        pltpu.VMEM((CHUNK_ROWS, 128), F32),
        pltpu.VMEM((CHUNK, L), BF16),
    ]
    return pl.pallas_call(
        kernel,
        out_shape=out_shape,
        in_specs=[VMEM] * len(operands),
        scratch_shapes=list(extra) + scratch,
        compiler_params=pltpu.CompilerParams(vmem_limit_bytes=VMEM_LIMIT),
        cost_estimate=pl.CostEstimate(
            flops=2 * chunks * CHUNK * L * 32, bytes_accessed=chunks * CHUNK * 256, transcendentals=0
        ),
        name="emission",
    )(*operands)


def products(total, terms_ref, pop_refs, offsets):
    me = lax.axis_index("blk") % HIGH

    def block(offset):
        return terms_ref[:, pl.ds(pl.multiple_of((me ^ offset) * LOW, LOW), LOW)]

    for pop_ref, own in zip(pop_refs, offsets):
        for i in range(0, len(own), 2):
            terms = jnp.concatenate([block(offset) for offset in own[i : i + 2]], axis=1)
            pop = pop_ref[:, i * LOW : i * LOW + terms.shape[1]]
            new = lax.dot_general(pop, terms, CONTRACT_LAST, preferred_element_type=F32)
            total = new if total is None else total + new
    return total


def early_kernel(terms_ref, *refs, offsets):
    refs[-1][...] = products(None, terms_ref, refs[:-1], offsets)


def image_kernel(slit_ref, terms_ref, given_ref, *refs, offsets):
    pop_refs, (out_ref, pad_ref) = refs[:-2], refs[-2:]
    cells, outputs = pop_refs[0].shape[0], out_ref.shape[2]
    total = products(given_ref[...], terms_ref, pop_refs, offsets)
    edge = 2 * REACH
    pad_ref[:8, :] = jnp.zeros((8, pad_ref.shape[1]), F32)
    pad_ref[8 + cells :, :] = jnp.zeros((8, pad_ref.shape[1]), F32)
    pad_ref[8 : 8 + cells, :outputs] = total[:, :outputs] + total[:, outputs : 2 * outputs]
    pad_ref[8 : 8 + cells, outputs : outputs + edge] = (
        total[:, 2 * outputs : 2 * outputs + edge] + total[:, 2 * outputs + edge :]
    )
    image = slit_ref[:, 0:1] * pad_ref[4 : 4 + cells, :]
    for tap in range(1, 9):
        image += slit_ref[:, tap : tap + 1] * pad_ref[4 + tap : 4 + tap + cells, :]
    lane = lax.broadcasted_iota(jnp.int32, (8, 128), 1)
    for place in range(cells // CELL_DEV):
        own = image[place * CELL_DEV : (place + 1) * CELL_DEV]
        out_ref[place, :CELL_DEV, :] = own[:, :outputs]
        moved = pltpu.roll(own[8:, outputs:], edge, 1)
        out_ref[place, CELL_DEV:, :] = jnp.where(lane < edge, own[:8, outputs:], moved)


def join(got):
    count, outputs = got.shape[0], got.shape[2]
    edge = got[:, CELL_DEV:, :]
    after = jnp.concatenate([edge[:-1, :, :REACH], edge[:-1, :, 2 * REACH : 3 * REACH]], axis=1)
    before = jnp.concatenate([edge[1:, :, REACH : 2 * REACH], edge[1:, :, 3 * REACH : 4 * REACH]], axis=1)
    image = got[:, :CELL_DEV, :]
    image += jnp.pad(after, ((1, 0), (0, 0), (0, outputs - REACH)))
    image += jnp.pad(before, ((0, 1), (0, 0), (outputs - REACH, 0)))
    return jnp.transpose(image, (1, 0, 2)).reshape(CELL_DEV, count * outputs)


def early_products(terms, pops, offsets):
    return pl.pallas_call(
        functools.partial(early_kernel, offsets=offsets),
        out_shape=jax.ShapeDtypeStruct((pops[0].shape[0], terms.shape[0]), F32),
        in_specs=[VMEM] * (1 + len(pops)),
        compiler_params=pltpu.CompilerParams(vmem_limit_bytes=VMEM_LIMIT),
        cost_estimate=pl.CostEstimate(flops=3 << 28, bytes_accessed=1 << 20, transcendentals=0),
        name="early",
    )(terms, *pops)


def slit_image(slit, terms, given, pops, offsets):
    cells, outputs = pops[0].shape[0], terms.shape[0] // 2 - 2 * REACH
    return pl.pallas_call(
        functools.partial(image_kernel, offsets=offsets),
        out_shape=jax.ShapeDtypeStruct((cells // CELL_DEV, CELL_DEV + 8, outputs), F32),
        in_specs=[VMEM] * (3 + len(pops)),
        scratch_shapes=[pltpu.VMEM((cells + 16, outputs + 128), F32)],
        compiler_params=pltpu.CompilerParams(vmem_limit_bytes=VMEM_LIMIT),
        cost_estimate=pl.CostEstimate(flops=1 << 28, bytes_accessed=1 << 20, transcendentals=0),
        name="image",
    )(slit, terms, given, *pops)


def swap(values, offset, count):
    return lax.ppermute(values, "blk", [(i, i ^ offset) for i in range(count)])


def body(pop_cells, cell_map, line_level, line_strength, inst_wave, inst_slit):
    count = lax.axis_size("blk")
    own_levels = pop_cells.shape[0]
    bins = line_level.shape[0] // LINES_BIN
    outputs, chunks = bins // BINS, bins // CHUNK
    cells = CELL_DEV * count
    hold = lax.optimization_barrier

    onehot = (cell_map[None, :] == jnp.arange(cells, dtype=jnp.int32)[:, None]).astype(BF16)
    pop = lax.dot_general(onehot, pop_cells, CONTRACT_LAST, preferred_element_type=F32).astype(BF16)
    if count > HIGH:
        sets = [list(range(i, count, HIGH)) for i in range(HIGH)]
        pop = lax.all_gather(pop, "blk", axis=1, tiled=True, axis_index_groups=sets)

    lines = (line_level.reshape(-1, 128), line_strength.reshape(-1, 128), tap_matrix(inst_wave.reshape(1, -1)))
    early = EARLY
    far = [swap(pop, k, count) for k in (4, 8, 12)]
    beside = swap(pop, 2, count)
    total = emission_call(
        functools.partial(first_kernel, chunks=range(early), own_levels=own_levels),
        jax.ShapeDtypeStruct((outputs + 2 * REACH, L), F32),
        lines,
        early,
    )
    far, beside, total = hold((far, beside, total))
    pair, beside = hold((jnp.concatenate(far[1:], axis=1), beside))
    across = swap(pair, 2, count)
    corner = swap(beside, 4, count)
    near = jnp.concatenate([pop, beside] + list(far), axis=1)
    near_pair = swap(near, 1, count)
    terms = emission_call(
        functools.partial(last_kernel, chunks=range(early, chunks), own_levels=own_levels),
        jax.ShapeDtypeStruct((2 * outputs + 4 * REACH, L), BF16),
        lines + (total,),
        chunks - early,
        [pltpu.VMEM((outputs + 2 * REACH, L), F32)],
    )
    across, corner, terms = hold((across, corner, terms))
    rest = jnp.concatenate([across, corner], axis=1)
    rest_pair = swap(rest, 1, count)
    first = early_products(terms, [near, near_pair, rest], [[0, 2, 4, 8, 12], [1, 3, 5, 9, 13], [10, 14, 6]])
    rest_pair, first = hold((rest_pair, first))
    image = slit_image(inst_slit.reshape(1, -1), terms, first, [rest_pair], [[11, 15, 7]])
    return join(lax.all_to_all(image, "blk", split_axis=0, concat_axis=0, tiled=True))


def solution(mesh):
    placed = (P("blk", "groups"), P(), P("blk"), P("blk"), P(), P())
    return jax.shard_map(
        body, mesh=mesh, in_specs=placed, out_specs=P(("groups", "blk"), None), check_vma=False
    )
```

```python
import functools

import jax
import jax.numpy as jnp
from jax import lax
from jax.experimental import pallas as pl
from jax.experimental.pallas import tpu as pltpu
from jax.sharding import PartitionSpec as P

L = 2048
LINES_BIN = 32
CELL_DEV = 16
LOW = 128
HIGH = L // LOW
BINS = 8
CHUNK = 256
REACH = 8
CHUNK_OUT = CHUNK // BINS
SPAN = CHUNK_OUT + 2 * REACH
CHUNK_ROWS = CHUNK * LINES_BIN // 128
TAP_WIDTH = 512
TAP_FLOPS = 1 << 32
UNROLL = 16
EARLY = 1
BF16 = jnp.bfloat16
F32 = jnp.float32
VMEM_LIMIT = 48 * 1024 * 1024
CONTRACT_LAST = (((1,), (1,)), ((), ()))
VMEM = pl.BlockSpec(memory_space=pltpu.VMEM)


def two_terms(values):
    first = values.astype(BF16)
    return first, (values - first.astype(F32)).astype(BF16)


def tap_kernel(wave_ref, out_ref, tap_ref):
    tap_ref[...] = jnp.zeros_like(tap_ref)
    tap_ref[:, : wave_ref.shape[1]] = jnp.broadcast_to(wave_ref[...], (8, wave_ref.shape[1]))
    base = jnp.concatenate([tap_ref[...]] * (SPAN // 8), axis=0)
    taps = pltpu.roll(base, TAP_WIDTH - 128, 1, stride=BINS, stride_axis=0)[:, :CHUNK]
    first, second = two_terms(taps)
    out_ref[:SPAN, :] = first
    out_ref[SPAN:, :] = second


def tap_matrix(wave):
    return pl.pallas_call(
        tap_kernel,
        out_shape=jax.ShapeDtypeStruct((2 * SPAN, CHUNK), BF16),
        in_specs=[VMEM],
        scratch_shapes=[pltpu.VMEM((8, TAP_WIDTH), F32)],
        compiler_params=pltpu.CompilerParams(vmem_limit_bytes=VMEM_LIMIT),
        cost_estimate=pl.CostEstimate(flops=TAP_FLOPS, bytes_accessed=1 << 16, transcendentals=0),
        name="taps",
    )(wave)


def emission(lines, own_levels, scratch):
    level_ref, strength_ref, first_row, rows = lines
    high_ref, low_ref, em_ref = scratch
    level = level_ref[first_row : first_row + rows, :].astype(jnp.int32)
    owner = level // own_levels
    row_bin = lax.broadcasted_iota(jnp.int32, (rows, 128), 0) % 2 * (128 // LINES_BIN)
    lane_bin = lax.broadcasted_iota(jnp.int32, (rows, 128), 1) // LINES_BIN
    high_ref[:rows, :] = (owner % HIGH * BINS + row_bin + lane_bin).astype(F32)
    low_ref[:rows, :] = (owner // HIGH * own_levels + level % own_levels).astype(F32)

    choices = [
        (lax.broadcasted_iota(jnp.int32, (16, 128), 0) + 16 * block).astype(F32).astype(BF16)
        for block in range(LOW // 16)
    ]
    zero = jnp.zeros((16, 128), BF16)
    one = jnp.ones((16, 128), BF16)

    def spread(ref, index):
        return jnp.broadcast_to(ref[pl.ds(index, 1), :], (16, 128)).astype(BF16)

    def half(index):
        high = spread(high_ref, index)
        low = spread(low_ref, index)
        strength = spread(strength_ref, first_row + index)
        a = jnp.concatenate([jnp.where(high == choice, strength, zero) for choice in choices], axis=0)
        b = jnp.concatenate([jnp.where(low == choice, one, zero) for choice in choices], axis=0)
        return a, b

    def group(index):
        a0, b0 = half(2 * index)
        a1, b1 = half(2 * index + 1)
        return lax.dot_general(
            jnp.concatenate([a0, a1], axis=1),
            jnp.concatenate([b0, b1], axis=1),
            CONTRACT_LAST,
            preferred_element_type=F32,
        )

    @pl.loop(0, rows // 4, unroll=UNROLL)
    def _(pair):
        x = group(2 * pair)
        y = group(2 * pair + 1)
        place = pl.ds(pl.multiple_of(16 * pair, 16), 16)
        for h in range(HIGH):
            own = slice(BINS * h, BINS * h + BINS)
            em_ref[place, h * LOW : (h + 1) * LOW] = jnp.concatenate([x[own], y[own]], axis=0).astype(BF16)


def blurred(taps, em):
    both = jnp.dot(taps, em, preferred_element_type=F32)
    return both[:SPAN] + both[SPAN:]


def add_chunks(total_ref, chunks, taps, level_ref, strength_ref, own_levels, scratch):
    for chunk in chunks:
        emission((level_ref, strength_ref, chunk * CHUNK_ROWS, CHUNK_ROWS), own_levels, scratch)
        place = slice(chunk * CHUNK_OUT, chunk * CHUNK_OUT + SPAN)
        total_ref[place, :] += blurred(taps, scratch[-1][...])


def first_kernel(level_ref, strength_ref, taps_ref, total_ref, *scratch, chunks, own_levels):
    total_ref[...] = jnp.zeros_like(total_ref)
    add_chunks(total_ref, chunks, taps_ref[...], level_ref, strength_ref, own_levels, scratch)


def last_kernel(
    level_ref, strength_ref, taps_ref, given_ref, out_ref, total_ref, *scratch, chunks, own_levels
):
    outputs = total_ref.shape[0] - 2 * REACH
    total_ref[...] = given_ref[...]
    add_chunks(total_ref, chunks, taps_ref[...], level_ref, strength_ref, own_levels, scratch)
    first, second = two_terms(total_ref[REACH : REACH + outputs, :])
    out_ref[:outputs, :] = first
    out_ref[outputs : 2 * outputs, :] = second
    edges = jnp.concatenate([total_ref[REACH + outputs :, :], total_ref[:REACH, :]], axis=0)
    first, second = two_terms(edges)
    out_ref[2 * outputs : 2 * outputs + 2 * REACH, :] = first
    out_ref[2 * outputs + 2 * REACH :, :] = second


def emission_call(kernel, out_shape, operands, chunks, extra=()):
    scratch = [
        pltpu.VMEM((CHUNK_ROWS, 128), F32),
        pltpu.VMEM((CHUNK_ROWS, 128), F32),
        pltpu.VMEM((CHUNK, L), BF16),
    ]
    return pl.pallas_call(
        kernel,
        out_shape=out_shape,
        in_specs=[VMEM] * len(operands),
        scratch_shapes=list(extra) + scratch,
        compiler_params=pltpu.CompilerParams(vmem_limit_bytes=VMEM_LIMIT),
        cost_estimate=pl.CostEstimate(
            flops=2 * chunks * CHUNK * L * 32, bytes_accessed=chunks * CHUNK * 256, transcendentals=0
        ),
        name="emission",
    )(*operands)


def products(total, terms_ref, pop_refs, offsets):
    me = lax.axis_index("blk") % HIGH

    def block(offset):
        return terms_ref[:, pl.ds(pl.multiple_of((me ^ offset) * LOW, LOW), LOW)]

    for pop_ref, own in zip(pop_refs, offsets):
        for i in range(0, len(own), 2):
            terms = jnp.concatenate([block(offset) for offset in own[i : i + 2]], axis=1)
            pop = pop_ref[:, i * LOW : i * LOW + terms.shape[1]]
            new = lax.dot_general(pop, terms, CONTRACT_LAST, preferred_element_type=F32)
            total = new if total is None else total + new
    return total


def early_kernel(terms_ref, *refs, offsets):
    refs[-1][...] = products(None, terms_ref, refs[:-1], offsets)


def image_kernel(slit_ref, terms_ref, given_ref, *refs, offsets):
    pop_refs, (out_ref, pad_ref) = refs[:-2], refs[-2:]
    cells, outputs = pop_refs[0].shape[0], out_ref.shape[2]
    total = products(given_ref[...], terms_ref, pop_refs, offsets)
    edge = 2 * REACH
    pad_ref[:8, :] = jnp.zeros((8, pad_ref.shape[1]), F32)
    pad_ref[8 + cells :, :] = jnp.zeros((8, pad_ref.shape[1]), F32)
    pad_ref[8 : 8 + cells, :outputs] = total[:, :outputs] + total[:, outputs : 2 * outputs]
    pad_ref[8 : 8 + cells, outputs : outputs + edge] = (
        total[:, 2 * outputs : 2 * outputs + edge] + total[:, 2 * outputs + edge :]
    )
    image = slit_ref[:, 0:1] * pad_ref[4 : 4 + cells, :]
    for tap in range(1, 9):
        image += slit_ref[:, tap : tap + 1] * pad_ref[4 + tap : 4 + tap + cells, :]
    lane = lax.broadcasted_iota(jnp.int32, (8, 128), 1)
    for place in range(cells // CELL_DEV):
        own = image[place * CELL_DEV : (place + 1) * CELL_DEV]
        out_ref[place, :CELL_DEV, :] = own[:, :outputs]
        moved = pltpu.roll(own[8:, outputs:], edge, 1)
        out_ref[place, CELL_DEV:, :] = jnp.where(lane < edge, own[:8, outputs:], moved)


def join(got):
    count, outputs = got.shape[0], got.shape[2]
    edge = got[:, CELL_DEV:, :]
    after = jnp.concatenate([edge[:-1, :, :REACH], edge[:-1, :, 2 * REACH : 3 * REACH]], axis=1)
    before = jnp.concatenate([edge[1:, :, REACH : 2 * REACH], edge[1:, :, 3 * REACH : 4 * REACH]], axis=1)
    image = got[:, :CELL_DEV, :]
    image += jnp.pad(after, ((1, 0), (0, 0), (0, outputs - REACH)))
    image += jnp.pad(before, ((0, 1), (0, 0), (outputs - REACH, 0)))
    return jnp.transpose(image, (1, 0, 2)).reshape(CELL_DEV, count * outputs)


def early_products(terms, pops, offsets):
    return pl.pallas_call(
        functools.partial(early_kernel, offsets=offsets),
        out_shape=jax.ShapeDtypeStruct((pops[0].shape[0], terms.shape[0]), F32),
        in_specs=[VMEM] * (1 + len(pops)),
        compiler_params=pltpu.CompilerParams(vmem_limit_bytes=VMEM_LIMIT),
        cost_estimate=pl.CostEstimate(flops=3 << 28, bytes_accessed=1 << 20, transcendentals=0),
        name="early",
    )(terms, *pops)


def slit_image(slit, terms, given, pops, offsets):
    cells, outputs = pops[0].shape[0], terms.shape[0] // 2 - 2 * REACH
    return pl.pallas_call(
        functools.partial(image_kernel, offsets=offsets),
        out_shape=jax.ShapeDtypeStruct((cells // CELL_DEV, CELL_DEV + 8, outputs), F32),
        in_specs=[VMEM] * (3 + len(pops)),
        scratch_shapes=[pltpu.VMEM((cells + 16, outputs + 128), F32)],
        compiler_params=pltpu.CompilerParams(vmem_limit_bytes=VMEM_LIMIT),
        cost_estimate=pl.CostEstimate(flops=1 << 28, bytes_accessed=1 << 20, transcendentals=0),
        name="image",
    )(slit, terms, given, *pops)


def swap(values, offset, count):
    return lax.ppermute(values, "blk", [(i, i ^ offset) for i in range(count)])


def body(pop_cells, cell_map, line_level, line_strength, inst_wave, inst_slit):
    count = lax.axis_size("blk")
    own_levels = pop_cells.shape[0]
    bins = line_level.shape[0] // LINES_BIN
    outputs, chunks = bins // BINS, bins // CHUNK
    cells = CELL_DEV * count
    hold = lax.optimization_barrier

    onehot = (cell_map[None, :] == jnp.arange(cells, dtype=jnp.int32)[:, None]).astype(BF16)
    onehot = hold(onehot)
    pop = lax.dot_general(onehot, pop_cells, CONTRACT_LAST, preferred_element_type=F32).astype(BF16)
    if count > HIGH:
        sets = [list(range(i, count, HIGH)) for i in range(HIGH)]
        pop = lax.all_gather(pop, "blk", axis=1, tiled=True, axis_index_groups=sets)

    lines = (line_level.reshape(-1, 128), line_strength.reshape(-1, 128), tap_matrix(inst_wave.reshape(1, -1)))
    early = EARLY
    far = [swap(pop, k, count) for k in (4, 8, 12)]
    beside = swap(pop, 2, count)
    total = emission_call(
        functools.partial(first_kernel, chunks=range(early), own_levels=own_levels),
        jax.ShapeDtypeStruct((outputs + 2 * REACH, L), F32),
        lines,
        early,
    )
    far, beside, total = hold((far, beside, total))
    pair, beside = hold((jnp.concatenate(far[1:], axis=1), beside))
    across = swap(pair, 2, count)
    corner = swap(beside, 4, count)
    near = jnp.concatenate([pop, beside] + list(far), axis=1)
    near_pair = swap(near, 1, count)
    terms = emission_call(
        functools.partial(last_kernel, chunks=range(early, chunks), own_levels=own_levels),
        jax.ShapeDtypeStruct((2 * outputs + 4 * REACH, L), BF16),
        lines + (total,),
        chunks - early,
        [pltpu.VMEM((outputs + 2 * REACH, L), F32)],
    )
    across, corner, terms = hold((across, corner, terms))
    rest = jnp.concatenate([across, corner], axis=1)
    rest_pair = swap(rest, 1, count)
    first = early_products(terms, [near, near_pair, rest], [[0, 2, 4, 8, 12], [1, 3, 5, 9, 13], [10, 14, 6]])
    rest_pair, first = hold((rest_pair, first))
    image = slit_image(inst_slit.reshape(1, -1), terms, first, [rest_pair], [[11, 15, 7]])
    return join(lax.all_to_all(image, "blk", split_axis=0, concat_axis=0, tiled=True))


def solution(mesh):
    placed = (P("blk", "groups"), P(), P("blk"), P("blk"), P(), P())
    return jax.shard_map(
        body, mesh=mesh, in_specs=placed, out_specs=P(("groups", "blk"), None), check_vma=False
    )
```
